32 devices in a mesh: row: 8 (over y, x, core), col: 4 (over z).
Axes of the slice: x: 2, y: 2, z: 4, core: 2. Of those that a mesh axis runs over, the one named last changes fastest.
Arguments:
- t_amps: float32 [8192, 8192], P('row', 'col'), may hold values from -0.05 to 0.05
- cholesky: float32 [8192, 2048], P(('row', 'col')), may hold values from -0.79549515 to 0.79549515
- eps_occ: float32 [8], replicated, may hold values from -2 to -0.3
- eps_vir: float32 [1024], replicated, may hold values from 0.2 to 4
Outputs:
- t_new: float32 [8192, 8192], P('row', 'col')
The draws below stay inside these ranges and needn't reach their ends.
All inputs are finite; a program needn't handle non-finite values.
Results may differ from the reference program's by a relative error of at most 0.000088.
Values sent between devices are 32-bit elements; how exact they have to be, the bound alone decides.
No kernel may reach another device: no remote copies, remote signals or barrier semaphores. Data moves between devices by JAX's collectives and lax.ppermute only.
A program may use at most 128 MiB of HBM per device.

```python
import jax
import jax.numpy as jnp
from jax import lax

OCC = 8
VIR = 1024
CHOL = 2048
OV = 8192
N_ROW = 8
N_COL = 4


def levels(own_key, extent, cuts, least, largest):
    gain = 1.0
    for dim, shards_of in cuts:
        steps = jax.random.uniform(jax.random.fold_in(jax.random.fold_in(own_key, 6), dim), (shards_of,), jnp.float32, least / len(cuts), largest / len(cuts))
        gain = gain * jnp.repeat(jnp.exp(steps), extent[dim] // shards_of).reshape((-1,) + (1,) * (len(extent) - 1 - dim))
    return gain


def gaussian(own_key, extent, deviation, most, shards=(), kind=jnp.bfloat16):
    level = levels(own_key, extent, shards, -0.22, 0.18) if shards else 1.0
    values = jax.random.normal(own_key, extent, jnp.float32) * deviation * level
    return jnp.minimum(jnp.maximum(values, -most), most).astype(kind)


def setup_inputs(seed: int = 0) -> dict:
    splits = jax.random.split(jax.random.key(seed), 5)
    return {
        "t_amps": gaussian(splits[0], (OV, OV), 0.008, 0.05, ((0, 8), (1, 4)), jnp.float32),
        "cholesky": gaussian(splits[1], (OV, CHOL), (4.5 * CHOL ** -0.5), 0.79549515, ((0, 32),), jnp.float32),
        "eps_occ": jnp.clip(jax.random.uniform(splits[2], (OCC,), jnp.float32, -2.0, -0.3), -2.0, -0.3),
        "eps_vir": jnp.clip(jax.random.uniform(splits[3], (VIR,), jnp.float32, 0.2, 4.0), 0.2, 4.0),
    }


def reference(t_amps, cholesky, eps_occ, eps_vir):
    blk = OV // (N_ROW * N_COL)
    tmat = t_amps.reshape(OV, N_COL, N_ROW, blk).transpose(0, 2, 1, 3).reshape(OV, OV)
    tl_prod = jnp.dot(tmat, cholesky, precision=lax.Precision.HIGHEST, preferred_element_type=jnp.float32)
    mixed = cholesky + tl_prod
    gaps = (eps_vir[None, :] - eps_occ[:, None]).reshape(OV)
    outer = jnp.dot(mixed, mixed.T, precision=lax.Precision.HIGHEST, preferred_element_type=jnp.float32)
    result = -outer / (gaps[:, None] + gaps[None, :])
    return result.reshape(OV, N_ROW, N_COL, blk).transpose(0, 2, 1, 3).reshape(OV, OV)
```

```python
import jax
import jax.numpy as jnp
from jax import lax
from jax.sharding import PartitionSpec as P

CHUNKS = 8
PARTS = 1
FACTOR_GROUPS = (1, 1, 2, 4)
LAG = 1
M_GROUPS = (4, 2, 2)
F32 = jnp.float32


def mul(a, b, dims):
    return lax.dot_general(
        a, b, (dims, ((), ())), precision=lax.Precision.HIGH, preferred_element_type=F32
    )


def ring_of(chips):
    if chips & (chips - 1) == 0:
        return [i ^ (i >> 1) for i in range(chips)]
    return list(range(chips))


def ring_gather(x, nrow, beside=None):
    chips = nrow // 2
    ring = ring_of(chips)
    blk, width = x.shape

    def shift(y, by):
        pairs = [
            (2 * ring[i] + k, 2 * ring[(i + by) % chips] + k) for i in range(chips) for k in range(2)
        ]
        return lax.ppermute(y, "row", pairs)

    got = {0: x}
    for step in range(1, chips // 2 + 1):
        if 2 * step < chips:
            got[chips - step] = shift(got[(chips - step + 1) % chips], 1)
            got[step] = shift(got[step - 1], -1)
            if step == 1:
                got, beside = lax.optimization_barrier((got, beside))
        else:
            half = blk // 2
            upper = shift(got[(chips - step + 1) % chips][:half], 1)
            lower = shift(got[step - 1][half:], -1)
            got[step] = jnp.concatenate([upper, lower], axis=0)
    mine = jnp.concatenate([got[i] for i in range(chips)], axis=0)
    other = lax.ppermute(mine, "row", [(i, i ^ 1) for i in range(nrow)])
    pieces = jnp.concatenate([mine, other], axis=0)
    place = {c: i for i, c in enumerate(ring)}
    table = []
    for r in range(nrow):
        near = [2 * ring[(place[r // 2] + i) % chips] for i in range(chips)]
        owner = [c + r % 2 for c in near] + [c + 1 - r % 2 for c in near]
        table.append([owner.index(i) for i in range(nrow)])
    source = jnp.asarray(table, jnp.int32)[lax.axis_index("row")]
    return jnp.concatenate(
        [lax.dynamic_slice_in_dim(pieces, source[i] * blk, blk, 0) for i in range(nrow)], axis=0
    ), beside


def row_gather(x, nrow, ring, beside=None):
    if ring and nrow % 2 == 0:
        return ring_gather(x, nrow, beside)
    return lax.all_gather(x, "row", axis=0, tiled=True), beside


def pick(index, options):
    value = options[-1]
    for i in range(len(options) - 2, -1, -1):
        if value is not options[i]:
            value = jnp.where(index == i, options[i], value)
    return value


def shards(t_amps, cholesky, eps_occ, eps_vir):
    rows, cols = t_amps.shape
    nrow, ncol = lax.axis_size("row"), lax.axis_size("col")
    blk, chol = cholesky.shape
    width = chol // CHUNKS
    r, z = lax.axis_index("row"), lax.axis_index("col")

    pair = jnp.arange(rows)[:, None] - z * blk
    t_one = t_amps + ((pair == jnp.arange(cols)[None, :] - r * blk) & (pair >= 0) & (pair < blk)).astype(F32)
    gaps = (eps_vir[None, :] - eps_occ[:, None]).reshape(nrow * rows)
    row_gap = lax.dynamic_slice_in_dim(gaps, r * rows, rows, 0)
    col_gap = lax.dynamic_slice_in_dim(gaps.reshape(nrow, ncol, blk), z, 1, 1).reshape(cols)

    factor, start = [], 0
    for i, count in enumerate(FACTOR_GROUPS):
        own = cholesky[:, start * width : (start + count) * width]
        if i == 0:
            l, (t_one, cholesky) = row_gather(own, nrow, True, (t_one, cholesky))
        else:
            l, _ = row_gather(own, nrow, False)
        factor += [(l, k * width) for k in range(count)]
        start += count

    part = width // PARTS
    units = CHUNKS * PARTS
    steps = units + ncol - 2
    tie = lax.optimization_barrier

    def multiply(c, t):
        l, offset = factor[c]
        return mul(t, l[:, offset : offset + width], ((1,), (0,)))

    product = {0: tie(multiply(0, t_one))}

    def unit(k):
        c, h = divmod(min(max(k, 0), units - 1), PARTS)
        c = min(c, max(product))
        return product[c][:, h * part : (h + 1) * part]

    up, down = [], []

    def terms(k):
        zero = jnp.zeros((rows, part), F32)
        return (
            unit(k),
            [zero] + [up[k + i - 1] for i in range(1, ncol)],
            [down[k + ncol - 2 - i] for i in range(ncol - 1)] + [zero],
        )

    parts, m_rows, m_cols, due = {}, {}, {}, {}

    def assemble(k, given):
        own, above, below = given
        parts[k] = own + pick(z, above) + pick(z, below)
        c, h = divmod(k, PARTS)
        if h < PARTS - 1:
            return None
        m_rows[c] = tie(jnp.concatenate([parts.pop(c * PARTS + i) for i in range(PARTS)], axis=1))
        return c

    def gather(c, beside=None):
        own = lax.dynamic_slice_in_dim(m_rows[c], z * blk, blk, 0)
        return row_gather(own, nrow, c == CHUNKS - 1, beside)

    def outer(out, rows_of, cols_of):
        a, b = jnp.concatenate(rows_of, axis=1), jnp.concatenate(cols_of, axis=1)
        term = mul(a, b, ((1,), (1,)))
        return term if out is None else out + term

    groups, start = [], 0
    for count in M_GROUPS:
        groups.append(range(start, start + count))
        start += count
    out, inverse = None, None
    for s in range(steps):
        above = pick(z, [unit(s - i) for i in range(ncol)])
        below = pick(z, [unit(s - (ncol - 1 - i)) for i in range(ncol)])
        if s > 0:
            above, below = above + up[-1], below + down[-1]
        k = s - (ncol - 1)
        given = terms(k) if k >= 0 else None
        ready = len(groups) > 1 and all(c in m_cols for c in groups[0])
        m_given = [m_rows[c] for c in groups[0]] if ready else None
        above, below, given, m_given, t, row_gap = tie((above, below, given, m_given, t_one, row_gap))
        live = [i for i in range(ncol - 1) if 0 <= s - i < units]
        up.append(lax.ppermute(above, "col", [(i, i + 1) for i in live]))
        down.append(lax.ppermute(below, "col", [(ncol - 1 - i, ncol - 2 - i) for i in live]))
        work = {}
        c = (s + 1) // PARTS
        if (s + 1) % PARTS == 0 and c < CHUNKS:
            work["product"] = multiply(c, t)
        if given is not None:
            done = assemble(k, given)
            if done is not None:
                due[s + LAG] = (done, gather(done)[0])
        if s in due:
            work["cols"] = due[s][1]
        if ready:
            out = outer(out, m_given, [m_cols[c] for c in groups.pop(0)])
            work["out"] = out
        if s == 1:
            work["inverse"] = -1.0 / (row_gap[:, None] + col_gap[None, :])
        up[-1], down[-1], work = tie((up[-1], down[-1], work))
        if "product" in work:
            product[c] = work["product"]
        if "cols" in work:
            m_cols[due.pop(s)[0]] = work["cols"]
        out = work.get("out", out)
        inverse = work.get("inverse", inverse)
    for k in range(steps - (ncol - 1), units):
        done = assemble(k, terms(k))
        if done is not None:
            m_cols[done] = gather(done)[0]
    for c, l in due.values():
        m_cols[c] = l
    for group in groups:
        out = outer(out, [m_rows[c] for c in group], [m_cols[c] for c in group])
    return out * inverse


def solution(mesh):
    in_specs = (P("row", "col"), P(("row", "col"), None), P(), P())
    out_specs = P("row", "col")
    return jax.shard_map(shards, mesh=mesh, in_specs=in_specs, out_specs=out_specs, check_vma=False)
```

```python
import functools

import jax
import jax.numpy as jnp
from jax import lax
from jax.experimental import pallas as pl
from jax.experimental.pallas import tpu as pltpu
from jax.sharding import PartitionSpec as P

CHUNKS = 8
GROUPS = (1, 2, 4)
FIRST = 4
LAG = 2
F32, BF16 = jnp.float32, jnp.bfloat16
VMEM = 40 * 1024 * 1024


def mul(a, b, dims):
    return lax.dot_general(
        a, b, (dims, ((), ())), precision=lax.Precision.HIGH, preferred_element_type=F32
    )


def ring_of(chips):
    if chips & (chips - 1) == 0:
        return [i ^ (i >> 1) for i in range(chips)]
    return list(range(chips))


def swap(x, nrow):
    return lax.ppermute(x, "row", [(i, i ^ 1) for i in range(nrow)])


def ring_gather(x, nrow, beside=None):
    chips = nrow // 2
    ring = ring_of(chips)
    blk = x.shape[0]

    def shift(y, by):
        pairs = [
            (2 * ring[i] + k, 2 * ring[(i + by) % chips] + k) for i in range(chips) for k in range(2)
        ]
        return lax.ppermute(y, "row", pairs)

    got = {0: x}
    for step in range(1, chips // 2 + 1):
        if 2 * step < chips:
            got[chips - step] = shift(got[(chips - step + 1) % chips], 1)
            got[step] = shift(got[step - 1], -1)
            if step == 1:
                got, beside = lax.optimization_barrier((got, beside))
        else:
            half = blk // 2
            upper = shift(got[(chips - step + 1) % chips][:half], 1)
            lower = shift(got[step - 1][half:], -1)
            got[step] = jnp.concatenate([upper, lower], axis=0)
    mine = jnp.concatenate([got[i] for i in range(chips)], axis=0)
    other = swap(mine, nrow)
    place = {c: i for i, c in enumerate(ring)}
    table = []
    for r in range(nrow):
        near = [2 * ring[(place[r // 2] + i) % chips] for i in range(chips)]
        owner = [c + r % 2 for c in near] + [c + 1 - r % 2 for c in near]
        table.append([owner.index(i) for i in range(nrow)])
    source = jnp.asarray(table, jnp.int32)[lax.axis_index("row")]
    return mine, other, source, beside


def row_gather(x):
    return lax.all_gather(x, "row", axis=0, tiled=True)


def pick(index, options):
    value = options[-1]
    for i in range(len(options) - 2, -1, -1):
        if value is not options[i]:
            value = jnp.where(index == i, options[i], value)
    return value


def split(x):
    hi = x.astype(BF16)
    return hi, (x - hi.astype(F32)).astype(BF16)


def update_kernel(count, nrow, ring, source, *refs):
    m, refs = refs[:count], refs[count:]
    c, refs = refs[: count - ring], refs[count - ring :]
    mine, other = refs[:2] if ring else (None, None)
    acc, row_gap, col_gap, out, wide = refs[2 * ring :]
    depth = m[0].shape[1]

    def widen(value, rows, k):
        hi, lo = split(value)
        for j, x in enumerate((hi, lo, hi)):
            wide[rows, (3 * k + j) * depth : (3 * k + j + 1) * depth] = x

    @pl.when(pl.program_id(0) == 0)
    def _():
        for k, x in enumerate(c):
            widen(x[...], slice(None), k)
        if ring:
            held = mine.shape[0]
            blk = 2 * held // nrow
            for i in range(nrow):
                rows = slice(i * blk, (i + 1) * blk)
                place = source[i] * blk

                @pl.when(place < held)
                def _():
                    widen(mine[pl.ds(pl.multiple_of(place, blk), blk), :], rows, count - 1)

                @pl.when(place >= held)
                def _():
                    widen(other[pl.ds(pl.multiple_of(place - held, blk), blk), :], rows, count - 1)

    left = []
    for x in m:
        hi, lo = split(x[...])
        left += [hi, hi, lo]
    term = lax.dot_general(
        jnp.concatenate(left, axis=1), wide[...], (((1,), (1,)), ((), ())), preferred_element_type=F32
    )
    total = acc[...] + term
    out[...] = -total / (row_gap[...] + col_gap[...]) if ring else total


def update(acc, m, c, ring=None, row_gap=None, col_gap=None):
    count = len(m)
    rows, depth = m[0].shape
    cols = acc.shape[1]
    step = min(rows, 256)
    fixed = lambda i, o: (0, 0)
    along = lambda i, o: (i, 0)
    if ring is None:
        source, pieces = jnp.zeros((8,), jnp.int32), []
        row_gap, col_gap = jnp.zeros((rows,), F32), jnp.zeros((cols,), F32)
    else:
        pieces, source = ring[:2], ring[2]
    return pl.pallas_call(
        functools.partial(update_kernel, count, source.shape[0], ring is not None),
        out_shape=jax.ShapeDtypeStruct((rows, cols), F32),
        grid_spec=pltpu.PrefetchScalarGridSpec(
            num_scalar_prefetch=1,
            grid=(rows // step,),
            in_specs=[pl.BlockSpec((step, depth), along)] * count
            + [pl.BlockSpec((cols, depth), fixed)] * len(c)
            + [pl.BlockSpec(x.shape, fixed) for x in pieces]
            + [
                pl.BlockSpec((step, cols), along),
                pl.BlockSpec((step, 1), along),
                pl.BlockSpec((1, cols), fixed),
            ],
            out_specs=pl.BlockSpec((step, cols), along),
            scratch_shapes=[pltpu.VMEM((cols, 3 * count * depth), BF16)],
        ),
        compiler_params=pltpu.CompilerParams(vmem_limit_bytes=VMEM),
        cost_estimate=pl.CostEstimate(
            flops=6 * rows * cols * depth * count, bytes_accessed=8 * rows * cols, transcendentals=0
        ),
        name="update" if ring is None else "finish",
    )(source, *m, *c, *pieces, acc, row_gap.reshape(rows, 1), col_gap.reshape(1, cols))


def shards(t_amps, cholesky, eps_occ, eps_vir):
    rows, cols = t_amps.shape
    nrow, ncol = lax.axis_size("row"), lax.axis_size("col")
    blk, chol = cholesky.shape
    width = chol // CHUNKS
    r, z = lax.axis_index("row"), lax.axis_index("col")
    tie = lax.optimization_barrier

    pair = jnp.arange(rows)[:, None] - z * blk
    t_one = t_amps + ((pair == jnp.arange(cols)[None, :] - r * blk) & (pair >= 0) & (pair < blk)).astype(F32)
    gaps = (eps_vir[None, :] - eps_occ[:, None]).reshape(nrow * rows)
    row_gap = lax.dynamic_slice_in_dim(gaps, r * rows, rows, 0)
    col_gap = lax.dynamic_slice_in_dim(gaps.reshape(nrow, ncol, blk), z, 1, 1).reshape(cols)

    mine, other, source, (t_one, cholesky) = ring_gather(cholesky[:, :width], nrow, (t_one, cholesky))
    pieces = jnp.concatenate([mine, other], axis=0)
    l = jnp.concatenate(
        [lax.dynamic_slice_in_dim(pieces, source[i] * blk, blk, 0) for i in range(nrow)], axis=0
    )
    factor, start = {0: (l, 0)}, 1
    for count in GROUPS:
        l = row_gather(cholesky[:, start * width : (start + count) * width])
        factor.update({start + k: (l, k * width) for k in range(count)})
        start += count

    def multiply(c, t):
        l, offset = factor[c]
        return mul(t, l[:, offset : offset + width], ((1,), (0,)))

    part_of = {0: tie(multiply(0, t_one))}
    steps = CHUNKS + ncol - 2

    def at(k):
        return part_of[min(max(k, 0), max(part_of))]

    def choose(s):
        return pick(z, [at(s - i) for i in range(ncol)]), pick(z, [at(s - (ncol - 1 - i)) for i in range(ncol)])

    up, down, m_rows, m_cols, due = [], [], {}, {}, {}

    def terms(c):
        return at(c), up[c : c + ncol - 1], down[c : c + ncol - 1]

    def assemble(given):
        term, above, below = given
        zero = jnp.zeros_like(term)
        return term + pick(z, [zero] + above) + pick(z, below[::-1] + [zero])

    def assemble_own(given):
        return assemble(jax.tree.map(lambda x: lax.dynamic_slice_in_dim(x, z * blk, blk, 0), given))

    def taken(chunks):
        return [m_rows[c] for c in chunks], [m_cols[c] for c in chunks]

    out, used = None, 0
    for s in range(steps):
        above, below = choose(s)
        if s > 0:
            above, below = above + up[-1], below + down[-1]
        c = s - (ncol - 1)
        given = terms(c) if c >= 0 else None
        span, kept = range(0), []
        if used == 0 and len(m_cols) >= FIRST:
            span = range(FIRST)
        elif used and len(m_cols) > used:
            span = range(used, len(m_cols))
        kept = [m_rows[k] for k in span]
        above, below, t, given, kept = tie((above, below, t_one, given, kept))
        live = [i for i in range(ncol - 1) if 0 <= s - i < CHUNKS]
        up.append(lax.ppermute(above, "col", [(i, i + 1) for i in live]))
        down.append(lax.ppermute(below, "col", [(ncol - 1 - i, ncol - 2 - i) for i in live]))
        work = {}
        if s + 1 < CHUNKS:
            part_of[s + 1] = multiply(s + 1, t)
            work["part"] = part_of[s + 1]
        if given is not None:
            due[s + LAG] = (c, row_gather(tie(assemble_own(given))))
            work["rows"] = assemble(given)
        if s in due:
            work["cols"] = due[s][1]
        if span:
            used = span[-1] + 1
            cols_of = [m_cols[k] for k in span]
            if out is None:
                a, b = jnp.concatenate(kept, axis=1), jnp.concatenate(cols_of, axis=1)
                out = mul(a, b, ((1,), (1,)))
            else:
                out = update(out, kept, cols_of)
            work["out"] = out
        up[-1], down[-1], work = tie((up[-1], down[-1], work))
        if "part" in work:
            part_of[s + 1] = work["part"]
        if given is not None:
            m_rows[c] = work["rows"]
        if "cols" in work:
            m_cols[due.pop(s)[0]] = work["cols"]
        out = work.get("out", out)
    end = CHUNKS - 1
    own, given = tie((assemble_own(terms(end)), terms(end)))
    ready = range(used, len(m_cols))
    for c, l in due.values():
        m_cols[c] = l
    if ready:
        out = update(out, *taken(ready))
    *ring, (out, m_rows[end]) = ring_gather(own, nrow, (out, assemble(given)))
    rest = range(ready.stop, end)
    return update(out, [m_rows[c] for c in [*rest, end]], [m_cols[c] for c in rest], ring, row_gap, col_gap)


def solution(mesh):
    in_specs = (P("row", "col"), P(("row", "col"), None), P(), P())
    out_specs = P("row", "col")
    return jax.shard_map(shards, mesh=mesh, in_specs=in_specs, out_specs=out_specs, check_vma=False)
```

```python
import functools

import jax
import jax.numpy as jnp
from jax import lax
from jax.experimental import pallas as pl
from jax.experimental.pallas import tpu as pltpu
from jax.sharding import PartitionSpec as P

CHUNKS = 8
GROUPS = (1, 2, 4)
FIRST = 4
LAG = 2
F32, BF16 = jnp.float32, jnp.bfloat16
VMEM = 48 * 1024 * 1024


def mul(a, b, dims):
    return lax.dot_general(
        a, b, (dims, ((), ())), precision=lax.Precision.HIGH, preferred_element_type=F32
    )


def ring_of(chips):
    if chips & (chips - 1) == 0:
        return [i ^ (i >> 1) for i in range(chips)]
    return list(range(chips))


def swap(x, nrow):
    return lax.ppermute(x, "row", [(i, i ^ 1) for i in range(nrow)])


def ring_gather(x, nrow, beside=None):
    chips = nrow // 2
    ring = ring_of(chips)
    blk = x.shape[0]

    def shift(y, by):
        pairs = [
            (2 * ring[i] + k, 2 * ring[(i + by) % chips] + k) for i in range(chips) for k in range(2)
        ]
        return lax.ppermute(y, "row", pairs)

    got = {0: x}
    for step in range(1, chips // 2 + 1):
        if 2 * step < chips:
            got[chips - step] = shift(got[(chips - step + 1) % chips], 1)
            got[step] = shift(got[step - 1], -1)
            if step == 1:
                got, beside = lax.optimization_barrier((got, beside))
        else:
            half = blk // 2
            upper = shift(got[(chips - step + 1) % chips][:half], 1)
            lower = shift(got[step - 1][half:], -1)
            got[step] = jnp.concatenate([upper, lower], axis=0)
    mine = jnp.concatenate([got[i] for i in range(chips)], axis=0)
    other = swap(mine, nrow)
    place = {c: i for i, c in enumerate(ring)}
    table = []
    for r in range(nrow):
        near = [2 * ring[(place[r // 2] + i) % chips] for i in range(chips)]
        owner = [c + r % 2 for c in near] + [c + 1 - r % 2 for c in near]
        table.append([owner.index(i) for i in range(nrow)])
    source = jnp.asarray(table, jnp.int32)[lax.axis_index("row")]
    return mine, other, source, beside


def row_gather(x):
    return lax.all_gather(x, "row", axis=0, tiled=True)


def pick(index, options):
    value = options[-1]
    for i in range(len(options) - 2, -1, -1):
        if value is not options[i]:
            value = jnp.where(index == i, options[i], value)
    return value


def split(x):
    hi = x.astype(BF16)
    return hi, (x - hi.astype(F32)).astype(BF16)


def update_kernel(count, nrow, ring, source, *refs):
    m, refs = refs[:count], refs[count:]
    c, refs = refs[: count - ring], refs[count - ring :]
    mine, other = refs[:2] if ring else (None, None)
    acc, row_gap, col_gap, out, wide = refs[2 * ring :]
    depth = m[0].shape[1]

    def widen(value, rows, k):
        hi, lo = split(value)
        for j, x in enumerate((hi, lo, hi)):
            wide[rows, (3 * k + j) * depth : (3 * k + j + 1) * depth] = x

    @pl.when(pl.program_id(0) == 0)
    def _():
        for k, x in enumerate(c):
            widen(x[...], slice(None), k)
        if ring:
            held = mine.shape[0]
            blk = 2 * held // nrow
            for i in range(nrow):
                rows = slice(i * blk, (i + 1) * blk)
                place = source[i] * blk

                @pl.when(place < held)
                def _():
                    widen(mine[pl.ds(pl.multiple_of(place, blk), blk), :], rows, count - 1)

                @pl.when(place >= held)
                def _():
                    widen(other[pl.ds(pl.multiple_of(place - held, blk), blk), :], rows, count - 1)

    left = []
    for x in m:
        hi, lo = split(x[...])
        left += [hi, hi, lo]
    term = lax.dot_general(
        jnp.concatenate(left, axis=1), wide[...], (((1,), (1,)), ((), ())), preferred_element_type=F32
    )
    total = acc[...] + term
    out[...] = -total / (row_gap[...] + col_gap[...]) if ring else total


def update(acc, m, c, ring=None, row_gap=None, col_gap=None):
    count = len(m)
    rows, depth = m[0].shape
    cols = acc.shape[1]
    step = min(rows, 512)
    fixed = lambda i, o: (0, 0)
    along = lambda i, o: (i, 0)
    if ring is None:
        source, pieces = jnp.zeros((8,), jnp.int32), []
        row_gap, col_gap = jnp.zeros((rows, 1), F32), jnp.zeros((1, cols), F32)
    else:
        pieces, source = ring[:2], ring[2]
    return pl.pallas_call(
        functools.partial(update_kernel, count, source.shape[0], ring is not None),
        out_shape=jax.ShapeDtypeStruct((rows, cols), F32),
        grid_spec=pltpu.PrefetchScalarGridSpec(
            num_scalar_prefetch=1,
            grid=(rows // step,),
            in_specs=[pl.BlockSpec((step, depth), along)] * count
            + [pl.BlockSpec((cols, depth), fixed)] * len(c)
            + [pl.BlockSpec(x.shape, fixed) for x in pieces]
            + [
                pl.BlockSpec((step, cols), along),
                pl.BlockSpec((step, 1), along),
                pl.BlockSpec((1, cols), fixed),
            ],
            out_specs=pl.BlockSpec((step, cols), along),
            scratch_shapes=[pltpu.VMEM((cols, 3 * count * depth), BF16)],
        ),
        compiler_params=pltpu.CompilerParams(vmem_limit_bytes=VMEM),
        cost_estimate=pl.CostEstimate(
            flops=6 * rows * cols * depth * count, bytes_accessed=8 * rows * cols, transcendentals=0
        ),
        name="update" if ring is None else "finish",
    )(source, *m, *c, *pieces, acc, row_gap, col_gap)


def shards(t_amps, cholesky, eps_occ, eps_vir):
    rows, cols = t_amps.shape
    nrow, ncol = lax.axis_size("row"), lax.axis_size("col")
    blk, chol = cholesky.shape
    width = chol // CHUNKS
    r, z = lax.axis_index("row"), lax.axis_index("col")
    tie = lax.optimization_barrier

    pair = jnp.arange(rows)[:, None] - z * blk
    t_one = t_amps + ((pair == jnp.arange(cols)[None, :] - r * blk) & (pair >= 0) & (pair < blk)).astype(F32)
    gaps = (eps_vir[None, :] - eps_occ[:, None]).reshape(nrow * rows)
    row_gap = lax.dynamic_slice_in_dim(gaps, r * rows, rows, 0).reshape(rows, 1)
    col_gap = lax.dynamic_slice_in_dim(gaps.reshape(nrow, ncol, blk), z, 1, 1).reshape(1, cols)

    mine, other, source, (t_one, cholesky) = ring_gather(cholesky[:, :width], nrow, (t_one, cholesky))
    pieces = jnp.concatenate([mine, other], axis=0)
    l = jnp.concatenate(
        [lax.dynamic_slice_in_dim(pieces, source[i] * blk, blk, 0) for i in range(nrow)], axis=0
    )
    factor, start = {0: (l, 0)}, 1
    for count in GROUPS:
        l = row_gather(cholesky[:, start * width : (start + count) * width])
        factor.update({start + k: (l, k * width) for k in range(count)})
        start += count

    def multiply(c, t):
        l, offset = factor[c]
        return mul(t, l[:, offset : offset + width], ((1,), (0,)))

    part_of = {0: tie(multiply(0, t_one))}
    steps = CHUNKS + ncol - 2

    def at(k):
        return part_of[min(max(k, 0), max(part_of))]

    def going_up(s):
        term = pick(z, [at(s - i) for i in range(ncol)])
        return term + up[-1] if up else term

    def going_down(s):
        term = pick(z, [at(s - (ncol - 1 - i)) for i in range(ncol)])
        return term + down[-1] if down else term

    up, down, partial, m_rows, m_cols, due = [], [], {}, {}, {}, {}

    def arrive(c, term, s, above, below):
        if 0 <= s - c <= ncol - 2:
            term = term + jnp.where(z == s - c + 1, above, 0.0) + jnp.where(z == c + ncol - 2 - s, below, 0.0)
        return term

    def own_rows(x):
        return lax.dynamic_slice_in_dim(x, z * blk, blk, 0)

    def taken(chunks):
        return [m_rows[c] for c in chunks], [m_cols[c] for c in chunks]

    out, used = None, 0
    above = going_up(0)
    for s in range(steps):
        below = going_down(s)
        c = s - (ncol - 1)
        came = (up[-1], down[-1]) if up else None
        if s < CHUNKS:
            partial[s] = part_of[s]
        span = range(0)
        if used == 0 and len(m_cols) >= FIRST:
            span = range(FIRST)
        elif used and len(m_cols) > used:
            span = range(used, len(m_cols))
        kept = [m_rows[k] for k in span]
        above, below, t, came, kept = tie((above, below, t_one, came, kept))
        live = [i for i in range(ncol - 1) if 0 <= s - i < CHUNKS]
        up.append(lax.ppermute(above, "col", [(i, i + 1) for i in live]))
        down.append(lax.ppermute(below, "col", [(ncol - 1 - i, ncol - 2 - i) for i in live]))
        work = {}
        if s + 1 < CHUNKS:
            work["part"] = multiply(s + 1, t)
        if came is not None:
            work["partial"] = {k: arrive(k, x, s - 1, *came) for k, x in partial.items() if k < s}
        if s == 1:
            work["gaps"] = (row_gap, col_gap)
        early = c >= 0 and s >= CHUNKS
        if early:
            own, partial[c], kept = tie((own_rows(work["partial"][c]), work["partial"].pop(c), kept))
            due[s + LAG] = (c, row_gather(own))
        if s in due:
            work["cols"] = due[s][1]
        if span:
            used = span[-1] + 1
            cols_of = [m_cols[k] for k in span]
            if out is None:
                a, b = jnp.concatenate(kept, axis=1), jnp.concatenate(cols_of, axis=1)
                out = mul(a, b, ((1,), (1,)))
            else:
                out = update(out, kept, cols_of)
            work["out"] = out
        up[-1], work = tie((up[-1], work))
        partial.update(work.get("partial", {}))
        row_gap, col_gap = work.get("gaps", (row_gap, col_gap))
        if "part" in work:
            part_of[s + 1] = work["part"]
        above = going_up(s + 1) if s + 1 < steps else None
        own = own_rows(partial[c]) if c >= 0 and not early else None
        down[-1], above, own = tie((down[-1], above, own))
        if c >= 0:
            m_rows[c] = partial.pop(c)
        if own is not None:
            due[s + LAG] = (c, row_gather(own))
        if "cols" in work:
            m_cols[due.pop(s)[0]] = work["cols"]
        out = work.get("out", out)
    end = CHUNKS - 1
    given = (partial[end], up[-1], down[-1])
    own, given = tie((arrive(end, own_rows(given[0]), steps - 1, own_rows(up[-1]), own_rows(down[-1])), given))
    ready = range(used, len(m_cols))
    for c, l in due.values():
        m_cols[c] = l
    if ready:
        out = update(out, *taken(ready))
    *ring, (out, m_rows[end]) = ring_gather(own, nrow, (out, arrive(end, given[0], steps - 1, *given[1:])))
    rest = range(ready.stop, end)
    return update(out, [m_rows[c] for c in [*rest, end]], [m_cols[c] for c in rest], ring, row_gap, col_gap)


def solution(mesh):
    in_specs = (P("row", "col"), P(("row", "col"), None), P(), P())
    out_specs = P("row", "col")
    return jax.shard_map(shards, mesh=mesh, in_specs=in_specs, out_specs=out_specs, check_vma=False)
```

```python
import functools

import jax
import jax.numpy as jnp
from jax import lax
from jax.experimental import pallas as pl
from jax.experimental.pallas import tpu as pltpu
from jax.sharding import PartitionSpec as P

CHUNKS = 8
GROUPS = (1, 2, 4)
FIRST = 4
LAG = 2
F32, BF16 = jnp.float32, jnp.bfloat16
VMEM = 48 * 1024 * 1024


def mul(a, b, dims):
    return lax.dot_general(
        a, b, (dims, ((), ())), precision=lax.Precision.HIGH, preferred_element_type=F32
    )


def ring_of(chips):
    if chips & (chips - 1) == 0:
        return [i ^ (i >> 1) for i in range(chips)]
    return list(range(chips))


def swap(x, nrow):
    return lax.ppermute(x, "row", [(i, i ^ 1) for i in range(nrow)])


def ring_gather(x, nrow, beside=None):
    chips = nrow // 2
    ring = ring_of(chips)
    blk = x.shape[0]

    def shift(y, by):
        pairs = [
            (2 * ring[i] + k, 2 * ring[(i + by) % chips] + k) for i in range(chips) for k in range(2)
        ]
        return lax.ppermute(y, "row", pairs)

    got = {0: x}
    for step in range(1, chips // 2 + 1):
        if 2 * step < chips:
            got[chips - step] = shift(got[(chips - step + 1) % chips], 1)
            got[step] = shift(got[step - 1], -1)
            if step == 1:
                got, beside = lax.optimization_barrier((got, beside))
        else:
            half = blk // 2
            upper = shift(got[(chips - step + 1) % chips][:half], 1)
            lower = shift(got[step - 1][half:], -1)
            got[step] = jnp.concatenate([upper, lower], axis=0)
    mine = jnp.concatenate([got[i] for i in range(chips)], axis=0)
    other = swap(mine, nrow)
    place = {c: i for i, c in enumerate(ring)}
    table = []
    for r in range(nrow):
        near = [2 * ring[(place[r // 2] + i) % chips] for i in range(chips)]
        owner = [c + r % 2 for c in near] + [c + 1 - r % 2 for c in near]
        table.append([owner.index(i) for i in range(nrow)])
    source = jnp.asarray(table, jnp.int32)[lax.axis_index("row")]
    return mine, other, source, beside


def row_gather(x):
    return lax.all_gather(x, "row", axis=0, tiled=True)


def pick(index, options):
    value = options[-1]
    for i in range(len(options) - 2, -1, -1):
        if value is not options[i]:
            value = jnp.where(index == i, options[i], value)
    return value


def split(x):
    hi = x.astype(BF16)
    return hi, (x - hi.astype(F32)).astype(BF16)


def update_kernel(count, nrow, ring, source, *refs):
    m, refs = refs[:count], refs[count:]
    c, refs = refs[: count - ring], refs[count - ring :]
    mine, other = refs[:2] if ring else (None, None)
    acc, row_gap, col_gap, out, wide = refs[2 if ring else 0 :]
    depth = m[0].shape[1]

    def widen(value, rows, k):
        hi, lo = split(value)
        for j, x in enumerate((hi, lo, hi)):
            wide[rows, (3 * k + j) * depth : (3 * k + j + 1) * depth] = x

    def widen_all(value, rows):
        for k in range(ring):
            widen(value[:, k * depth : (k + 1) * depth], rows, count - ring + k)

    @pl.when(pl.program_id(0) == 0)
    def _():
        for k, x in enumerate(c):
            widen(x[...], slice(None), k)
        if ring:
            held = mine.shape[0]
            blk = 2 * held // nrow
            for i in range(nrow):
                rows = slice(i * blk, (i + 1) * blk)
                place = source[i] * blk

                @pl.when(place < held)
                def _():
                    widen_all(mine[pl.ds(pl.multiple_of(place, blk), blk), :], rows)

                @pl.when(place >= held)
                def _():
                    widen_all(other[pl.ds(pl.multiple_of(place - held, blk), blk), :], rows)

    left = []
    for x in m:
        hi, lo = split(x[...])
        left += [hi, hi, lo]
    term = lax.dot_general(
        jnp.concatenate(left, axis=1), wide[...], (((1,), (1,)), ((), ())), preferred_element_type=F32
    )
    total = acc[...] + term
    out[...] = -total / (row_gap[...] + col_gap[...]) if ring else total


def update(acc, m, c, ring=None, row_gap=None, col_gap=None):
    count = len(m)
    rows, depth = m[0].shape
    cols = acc.shape[1]
    step = min(rows, 512)
    fixed = lambda i, o: (0, 0)
    along = lambda i, o: (i, 0)
    if ring is None:
        source, pieces = jnp.zeros((8,), jnp.int32), []
        row_gap, col_gap = jnp.zeros((rows, 1), F32), jnp.zeros((1, cols), F32)
    else:
        pieces, source = ring[:2], ring[2]
    return pl.pallas_call(
        functools.partial(update_kernel, count, source.shape[0], count - len(c)),
        out_shape=jax.ShapeDtypeStruct((rows, cols), F32),
        grid_spec=pltpu.PrefetchScalarGridSpec(
            num_scalar_prefetch=1,
            grid=(rows // step,),
            in_specs=[pl.BlockSpec((step, depth), along)] * count
            + [pl.BlockSpec((cols, depth), fixed)] * len(c)
            + [pl.BlockSpec(x.shape, fixed) for x in pieces]
            + [
                pl.BlockSpec((step, cols), along),
                pl.BlockSpec((step, 1), along),
                pl.BlockSpec((1, cols), fixed),
            ],
            out_specs=pl.BlockSpec((step, cols), along),
            scratch_shapes=[pltpu.VMEM((cols, 3 * count * depth), BF16)],
        ),
        compiler_params=pltpu.CompilerParams(vmem_limit_bytes=VMEM),
        cost_estimate=pl.CostEstimate(
            flops=6 * rows * cols * depth * count, bytes_accessed=8 * rows * cols, transcendentals=0
        ),
        name="update" if ring is None else "finish",
    )(source, *m, *c, *pieces, acc, row_gap, col_gap)


def shards(t_amps, cholesky, eps_occ, eps_vir):
    rows, cols = t_amps.shape
    nrow, ncol = lax.axis_size("row"), lax.axis_size("col")
    blk, chol = cholesky.shape
    width = chol // CHUNKS
    r, z = lax.axis_index("row"), lax.axis_index("col")
    tie = lax.optimization_barrier

    pair = jnp.arange(rows)[:, None] - z * blk
    t_one = t_amps + ((pair == jnp.arange(cols)[None, :] - r * blk) & (pair >= 0) & (pair < blk)).astype(F32)
    gaps = (eps_vir[None, :] - eps_occ[:, None]).reshape(nrow * rows)
    row_gap = lax.dynamic_slice_in_dim(gaps, r * rows, rows, 0).reshape(rows, 1)
    col_gap = lax.dynamic_slice_in_dim(gaps.reshape(nrow, ncol, blk), z, 1, 1).reshape(1, cols)

    mine, other, source, (t_one, cholesky) = ring_gather(cholesky[:, :width], nrow, (t_one, cholesky))
    pieces = jnp.concatenate([mine, other], axis=0)
    l = jnp.concatenate(
        [lax.dynamic_slice_in_dim(pieces, source[i] * blk, blk, 0) for i in range(nrow)], axis=0
    )
    factor, start = {0: (l, 0)}, 1
    for count in GROUPS:
        l = row_gather(cholesky[:, start * width : (start + count) * width])
        factor.update({start + k: (l, k * width) for k in range(count)})
        start += count

    def multiply(c, t):
        l, offset = factor[c]
        return mul(t, l[:, offset : offset + width], ((1,), (0,)))

    part_of = {0: tie(multiply(0, t_one))}
    steps = CHUNKS + ncol - 2

    def at(k):
        return part_of[min(max(k, 0), max(part_of))]

    def going_up(s):
        term = pick(z, [at(s - i) for i in range(ncol)])
        return term + up[-1] if up else term

    def going_down(s):
        term = pick(z, [at(s - (ncol - 1 - i)) for i in range(ncol)])
        return term + down[-1] if down else term

    up, down, partial, m_rows, m_cols, due = [], [], {}, {}, {}, {}

    def arrive(c, term, s, above, below):
        if 0 <= s - c <= ncol - 2:
            term = term + jnp.where(z == s - c + 1, above, 0.0) + jnp.where(z == c + ncol - 2 - s, below, 0.0)
        return term

    def own_rows(x):
        return lax.dynamic_slice_in_dim(x, z * blk, blk, 0)

    def taken(chunks):
        return [m_rows[c] for c in chunks], [m_cols[c] for c in chunks]

    out, used = None, 0
    above = going_up(0)
    for s in range(steps):
        below = going_down(s)
        c = s - (ncol - 1)
        came = (up[-1], down[-1]) if up else None
        if s < CHUNKS:
            partial[s] = part_of[s]
        span = range(0)
        if used == 0 and len(m_cols) >= FIRST:
            span = range(FIRST)
        elif used and len(m_cols) > used:
            span = range(used, len(m_cols))
        kept = [m_rows[k] for k in span]
        above, below, t, came, kept = tie((above, below, t_one, came, kept))
        live = [i for i in range(ncol - 1) if 0 <= s - i < CHUNKS]
        up.append(lax.ppermute(above, "col", [(i, i + 1) for i in live]))
        down.append(lax.ppermute(below, "col", [(ncol - 1 - i, ncol - 2 - i) for i in live]))
        work = {}
        if s + 1 < CHUNKS:
            work["part"] = multiply(s + 1, t)
        if came is not None:
            work["partial"] = {k: arrive(k, x, s - 1, *came) for k, x in partial.items() if k < s}
        if s == 1:
            work["gaps"] = (row_gap, col_gap)
        if s in due:
            work["cols"] = due[s][1]
        if span:
            used = span[-1] + 1
            cols_of = [m_cols[k] for k in span]
            if out is None:
                a, b = jnp.concatenate(kept, axis=1), jnp.concatenate(cols_of, axis=1)
                out = mul(a, b, ((1,), (1,)))
            else:
                out = update(out, kept, cols_of)
            work["out"] = out
        up[-1], work = tie((up[-1], work))
        partial.update(work.get("partial", {}))
        row_gap, col_gap = work.get("gaps", (row_gap, col_gap))
        if "part" in work:
            part_of[s + 1] = work["part"]
        above = going_up(s + 1) if s + 1 < steps else None
        own = own_rows(partial[c]) if 0 <= c and s < steps - 1 else None
        down[-1], above, own = tie((down[-1], above, own))
        if c >= 0:
            m_rows[c] = partial.pop(c)
        if own is not None:
            due[s + LAG] = (c, row_gather(own))
        if "cols" in work:
            m_cols[due.pop(s)[0]] = work["cols"]
        out = work.get("out", out)
    end = CHUNKS - 1
    given = (partial[end], up[-1], down[-1])
    own = arrive(end, own_rows(given[0]), steps - 1, own_rows(up[-1]), own_rows(down[-1]))
    own, given = tie((jnp.concatenate([own_rows(m_rows[end - 1]), own], axis=1), given))
    for c, l in due.values():
        m_cols[c] = l
    *ring, out = ring_gather(own, nrow, update(out, *taken(range(used, end - 2))))
    m_rows[end] = arrive(end, given[0], steps - 1, *given[1:])
    return update(out, [m_rows[c] for c in range(end - 2, end + 1)], [m_cols[end - 2]], ring, row_gap, col_gap)


def solution(mesh):
    in_specs = (P("row", "col"), P(("row", "col"), None), P(), P())
    out_specs = P("row", "col")
    return jax.shard_map(shards, mesh=mesh, in_specs=in_specs, out_specs=out_specs, check_vma=False)
```

```python
import functools

import jax
import jax.numpy as jnp
from jax import lax
from jax.experimental import pallas as pl
from jax.experimental.pallas import tpu as pltpu
from jax.sharding import PartitionSpec as P

CHUNKS = 8
GROUPS = (1, 2, 4)
FIRST = 4
LAG = 2
F32, BF16 = jnp.float32, jnp.bfloat16
VMEM = 48 * 1024 * 1024
LANES = 128


def mul(a, b, dims):
    return lax.dot_general(
        a, b, (dims, ((), ())), precision=lax.Precision.HIGH, preferred_element_type=F32
    )


def ring_of(chips):
    if chips & (chips - 1) == 0:
        return [i ^ (i >> 1) for i in range(chips)]
    return list(range(chips))


def swap(x, nrow):
    return lax.ppermute(x, "row", [(i, i ^ 1) for i in range(nrow)])


def ring_gather(x, nrow, beside=None):
    chips = nrow // 2
    ring = ring_of(chips)
    blk = x.shape[0]

    def shift(y, by):
        pairs = [
            (2 * ring[i] + k, 2 * ring[(i + by) % chips] + k) for i in range(chips) for k in range(2)
        ]
        return lax.ppermute(y, "row", pairs)

    got = {0: x}
    for step in range(1, chips // 2 + 1):
        if 2 * step < chips:
            got[chips - step] = shift(got[(chips - step + 1) % chips], 1)
            got[step] = shift(got[step - 1], -1)
            if step == 1:
                got, beside = lax.optimization_barrier((got, beside))
        else:
            half = blk // 2
            upper = shift(got[(chips - step + 1) % chips][:half], 1)
            lower = shift(got[step - 1][half:], -1)
            got[step] = jnp.concatenate([upper, lower], axis=0)
    mine = jnp.concatenate([got[i] for i in range(chips)], axis=0)
    other = swap(mine, nrow)
    place = {c: i for i, c in enumerate(ring)}
    table = []
    for r in range(nrow):
        near = [2 * ring[(place[r // 2] + i) % chips] for i in range(chips)]
        owner = [c + r % 2 for c in near] + [c + 1 - r % 2 for c in near]
        table.append([owner.index(i) for i in range(nrow)])
    source = jnp.asarray(table, jnp.int32)[lax.axis_index("row")]
    return mine, other, source, beside


def row_gather(x):
    return lax.all_gather(x, "row", axis=0, tiled=True)


def pick(index, options):
    value = options[-1]
    for i in range(len(options) - 2, -1, -1):
        if value is not options[i]:
            value = jnp.where(index == i, options[i], value)
    return value


def split(x):
    hi = x.astype(BF16)
    return hi, (x - hi.astype(F32)).astype(BF16)


def update_kernel(count, nrow, ring, source, *refs):
    m, refs = refs[:count], refs[count:]
    c, refs = refs[: count - ring], refs[count - ring :]
    mine, other = refs[:2] if ring else (None, None)
    acc, row_gap, col_gap, out, wide = refs[2 if ring else 0 :]
    depth = m[0].shape[1]

    def widen(value, rows, k):
        hi, lo = split(value)
        for j, x in enumerate((hi, lo, hi)):
            wide[rows, (3 * k + j) * depth : (3 * k + j + 1) * depth] = x

    def widen_all(value, rows):
        for k in range(ring):
            widen(value[:, k * depth : (k + 1) * depth], rows, count - ring + k)

    @pl.when(pl.program_id(0) == 0)
    def _():
        for k, x in enumerate(c):
            widen(x[...], slice(None), k)
        if ring:
            held = mine.shape[0]
            blk = 2 * held // nrow
            for i in range(nrow):
                rows = slice(i * blk, (i + 1) * blk)
                place = source[i] * blk

                @pl.when(place < held)
                def _():
                    widen_all(mine[pl.ds(pl.multiple_of(place, blk), blk), :], rows)

                @pl.when(place >= held)
                def _():
                    widen_all(other[pl.ds(pl.multiple_of(place - held, blk), blk), :], rows)

    left = []
    for x in m:
        hi, lo = split(x[...])
        left += [hi, hi, lo]
    term = lax.dot_general(
        jnp.concatenate(left, axis=1), wide[...], (((1,), (1,)), ((), ())), preferred_element_type=F32
    )
    total = acc[...] + term
    out[...] = -total / (row_gap[:, :1] + col_gap[...]) if ring else total


def update(acc, m, c, ring=None, row_gap=None, col_gap=None):
    count = len(m)
    rows, depth = m[0].shape
    cols = acc.shape[1]
    step = min(rows, 512 if ring is None else 256)
    fixed = lambda i, o: (0, 0)
    along = lambda i, o: (i, 0)
    if ring is None:
        source, pieces = jnp.zeros((8,), jnp.int32), []
        row_gap, col_gap = jnp.zeros((rows, LANES), F32), jnp.zeros((1, cols), F32)
    else:
        pieces, source = ring[:2], ring[2]
    return pl.pallas_call(
        functools.partial(update_kernel, count, source.shape[0], count - len(c)),
        out_shape=jax.ShapeDtypeStruct((rows, cols), F32),
        grid_spec=pltpu.PrefetchScalarGridSpec(
            num_scalar_prefetch=1,
            grid=(rows // step,),
            in_specs=[pl.BlockSpec((step, depth), along)] * count
            + [pl.BlockSpec((cols, depth), fixed)] * len(c)
            + [pl.BlockSpec(x.shape, fixed) for x in pieces]
            + [
                pl.BlockSpec((step, cols), along),
                pl.BlockSpec((step, LANES), along),
                pl.BlockSpec((1, cols), fixed),
            ],
            out_specs=pl.BlockSpec((step, cols), along),
            scratch_shapes=[pltpu.VMEM((cols, 3 * count * depth), BF16)],
        ),
        compiler_params=pltpu.CompilerParams(vmem_limit_bytes=VMEM),
        cost_estimate=pl.CostEstimate(
            flops=6 * rows * cols * depth * count, bytes_accessed=8 * rows * cols, transcendentals=0
        ),
        name="update" if ring is None else "finish",
    )(source, *m, *c, *pieces, acc, row_gap, col_gap)


def shards(t_amps, cholesky, eps_occ, eps_vir):
    rows, cols = t_amps.shape
    nrow, ncol = lax.axis_size("row"), lax.axis_size("col")
    blk, chol = cholesky.shape
    width = chol // CHUNKS
    r, z = lax.axis_index("row"), lax.axis_index("col")
    tie = lax.optimization_barrier

    pair = jnp.arange(rows)[:, None] - z * blk
    t_one = t_amps + ((pair == jnp.arange(cols)[None, :] - r * blk) & (pair >= 0) & (pair < blk)).astype(F32)
    gaps = (eps_vir[None, :] - eps_occ[:, None]).reshape(nrow * rows)
    row_gap = lax.dynamic_slice_in_dim(gaps, r * rows, rows, 0)
    row_gap = jnp.broadcast_to(row_gap[:, None], (rows, LANES))
    col_gap = lax.dynamic_slice_in_dim(gaps.reshape(nrow, ncol, blk), z, 1, 1).reshape(1, cols)

    mine, other, source, (t_one, cholesky) = ring_gather(cholesky[:, :width], nrow, (t_one, cholesky))
    pieces = jnp.concatenate([mine, other], axis=0)
    l = jnp.concatenate(
        [lax.dynamic_slice_in_dim(pieces, source[i] * blk, blk, 0) for i in range(nrow)], axis=0
    )
    factor, start = {0: (l, 0)}, 1
    for count in GROUPS:
        l = row_gather(cholesky[:, start * width : (start + count) * width])
        factor.update({start + k: (l, k * width) for k in range(count)})
        start += count

    def multiply(c, t):
        l, offset = factor[c]
        return mul(t, l[:, offset : offset + width], ((1,), (0,)))

    part_of = {0: tie(multiply(0, t_one))}
    steps = CHUNKS + ncol - 2

    def at(k):
        return part_of[min(max(k, 0), max(part_of))]

    def going_up(s):
        term = pick(z, [at(s - i) for i in range(ncol)])
        return term + up[-1] if up else term

    def going_down(s):
        term = pick(z, [at(s - (ncol - 1 - i)) for i in range(ncol)])
        return term + down[-1] if down else term

    up, down, partial, m_rows, m_cols, due = [], [], {}, {}, {}, {}

    def arrive(c, term, s, above, below):
        if 0 <= s - c <= ncol - 2:
            term = term + jnp.where(z == s - c + 1, above, 0.0) + jnp.where(z == c + ncol - 2 - s, below, 0.0)
        return term

    def own_rows(x):
        return lax.dynamic_slice_in_dim(x, z * blk, blk, 0)

    def taken(chunks):
        return [m_rows[c] for c in chunks], [m_cols[c] for c in chunks]

    out, used = None, 0
    above = going_up(0)
    for s in range(steps):
        below = going_down(s)
        c = s - (ncol - 1)
        came = (up[-1], down[-1]) if up else None
        if s < CHUNKS:
            partial[s] = part_of[s]
        span = range(0)
        if used == 0 and len(m_cols) >= FIRST:
            span = range(FIRST)
        elif used and len(m_cols) > used:
            span = range(used, len(m_cols))
        kept = [m_rows[k] for k in span]
        above, below, t, came, kept = tie((above, below, t_one, came, kept))
        live = [i for i in range(ncol - 1) if 0 <= s - i < CHUNKS]
        up.append(lax.ppermute(above, "col", [(i, i + 1) for i in live]))
        down.append(lax.ppermute(below, "col", [(ncol - 1 - i, ncol - 2 - i) for i in live]))
        work = {}
        if s + 1 < CHUNKS:
            work["part"] = multiply(s + 1, t)
        if came is not None:
            work["partial"] = {k: arrive(k, x, s - 1, *came) for k, x in partial.items() if k < s}
        if s == 1:
            work["gaps"] = (row_gap, col_gap)
        if s in due:
            work["cols"] = due[s][1]
        if span:
            used = span[-1] + 1
            cols_of = [m_cols[k] for k in span]
            if out is None:
                a, b = jnp.concatenate(kept, axis=1), jnp.concatenate(cols_of, axis=1)
                out = mul(a, b, ((1,), (1,)))
            else:
                out = update(out, kept, cols_of)
            work["out"] = out
        up[-1], work = tie((up[-1], work))
        partial.update(work.get("partial", {}))
        row_gap, col_gap = work.get("gaps", (row_gap, col_gap))
        if "part" in work:
            part_of[s + 1] = work["part"]
        above = going_up(s + 1) if s + 1 < steps else None
        own = own_rows(partial[c]) if 0 <= c and s < steps - 1 else None
        down[-1], above, own = tie((down[-1], above, own))
        if c >= 0:
            m_rows[c] = partial.pop(c)
        if own is not None:
            due[s + LAG] = (c, row_gather(own))
        if "cols" in work:
            m_cols[due.pop(s)[0]] = work["cols"]
        out = work.get("out", out)
    end = CHUNKS - 1
    given = (partial[end], up[-1], down[-1])
    own = arrive(end, own_rows(given[0]), steps - 1, own_rows(up[-1]), own_rows(down[-1]))
    own, given = tie((jnp.concatenate([own_rows(m_rows[end - 1]), own], axis=1), given))
    for c, l in due.values():
        m_cols[c] = l
    *ring, out = ring_gather(own, nrow, update(out, *taken(range(used, end - 2))))
    m_rows[end] = arrive(end, given[0], steps - 1, *given[1:])
    return update(out, [m_rows[c] for c in range(end - 2, end + 1)], [m_cols[end - 2]], ring, row_gap, col_gap)


def solution(mesh):
    in_specs = (P("row", "col"), P(("row", "col"), None), P(), P())
    out_specs = P("row", "col")
    return jax.shard_map(shards, mesh=mesh, in_specs=in_specs, out_specs=out_specs, check_vma=False)
```

```python
import functools

import jax
import jax.numpy as jnp
from jax import lax
from jax.experimental import pallas as pl
from jax.experimental.pallas import tpu as pltpu
from jax.sharding import PartitionSpec as P

CHUNKS = 8
GROUPS = (1, 1, 2, 3)
FIRST = 4
LAG = 2
F32, BF16 = jnp.float32, jnp.bfloat16
VMEM = 48 * 1024 * 1024


def mul(a, b, dims):
    return lax.dot_general(
        a, b, (dims, ((), ())), precision=lax.Precision.HIGH, preferred_element_type=F32
    )


def ring_of(chips):
    if chips & (chips - 1) == 0:
        return [i ^ (i >> 1) for i in range(chips)]
    return list(range(chips))


def swap(x, nrow):
    return lax.ppermute(x, "row", [(i, i ^ 1) for i in range(nrow)])


def ring_gather(x, nrow, beside=None):
    chips = nrow // 2
    ring = ring_of(chips)
    blk = x.shape[0]

    def shift(y, by):
        pairs = [
            (2 * ring[i] + k, 2 * ring[(i + by) % chips] + k) for i in range(chips) for k in range(2)
        ]
        return lax.ppermute(y, "row", pairs)

    got = {0: x}
    for step in range(1, chips // 2 + 1):
        if 2 * step < chips:
            got[chips - step] = shift(got[(chips - step + 1) % chips], 1)
            got[step] = shift(got[step - 1], -1)
            if step == 1:
                got, beside = lax.optimization_barrier((got, beside))
        else:
            half = blk // 2
            upper = shift(got[(chips - step + 1) % chips][:half], 1)
            lower = shift(got[step - 1][half:], -1)
            got[step] = jnp.concatenate([upper, lower], axis=0)
    mine = jnp.concatenate([got[i] for i in range(chips)], axis=0)
    other = swap(mine, nrow)
    place = {c: i for i, c in enumerate(ring)}
    table = []
    for r in range(nrow):
        near = [2 * ring[(place[r // 2] + i) % chips] for i in range(chips)]
        owner = [c + r % 2 for c in near] + [c + 1 - r % 2 for c in near]
        table.append([owner.index(i) for i in range(nrow)])
    source = jnp.asarray(table, jnp.int32)[lax.axis_index("row")]
    return mine, other, source, beside


def row_gather(x):
    return lax.all_gather(x, "row", axis=0, tiled=True)


def pick(index, options):
    value = options[-1]
    for i in range(len(options) - 2, -1, -1):
        if value is not options[i]:
            value = jnp.where(index == i, options[i], value)
    return value


def split(x):
    hi = x.astype(BF16)
    return hi, (x - hi.astype(F32)).astype(BF16)


def update_kernel(count, nrow, ring, source, *refs):
    m, refs = refs[:count], refs[count:]
    c, refs = refs[: count - ring], refs[count - ring :]
    mine, other = refs[:2] if ring else (None, None)
    acc, row_gap, col_gap, out, wide = refs[2 if ring else 0 :]
    depth = m[0].shape[1]

    def widen(value, rows, k):
        hi, lo = split(value)
        for j, x in enumerate((hi, lo, hi)):
            wide[rows, (3 * k + j) * depth : (3 * k + j + 1) * depth] = x

    def widen_all(value, rows):
        for k in range(ring):
            widen(value[:, k * depth : (k + 1) * depth], rows, count - ring + k)

    @pl.when(pl.program_id(0) == 0)
    def _():
        for k, x in enumerate(c):
            widen(x[...], slice(None), k)
        if ring:
            held = mine.shape[0]
            blk = 2 * held // nrow
            for i in range(nrow):
                rows = slice(i * blk, (i + 1) * blk)
                place = source[i] * blk

                @pl.when(place < held)
                def _():
                    widen_all(mine[pl.ds(pl.multiple_of(place, blk), blk), :], rows)

                @pl.when(place >= held)
                def _():
                    widen_all(other[pl.ds(pl.multiple_of(place - held, blk), blk), :], rows)

    left = []
    for x in m:
        hi, lo = split(x[...])
        left += [hi, hi, lo]
    term = lax.dot_general(
        jnp.concatenate(left, axis=1), wide[...], (((1,), (1,)), ((), ())), preferred_element_type=F32
    )
    total = acc[...] + term
    out[...] = -total / (row_gap[...] + col_gap[...]) if ring else total


def update(acc, m, c, ring=None, row_gap=None, col_gap=None):
    count = len(m)
    rows, depth = m[0].shape
    cols = acc.shape[1]
    step = min(rows, 512)
    fixed = lambda i, o: (0, 0)
    along = lambda i, o: (i, 0)
    if ring is None:
        source, pieces = jnp.zeros((8,), jnp.int32), []
        row_gap, col_gap = jnp.zeros((rows, 1), F32), jnp.zeros((1, cols), F32)
    else:
        pieces, source = ring[:2], ring[2]
    return pl.pallas_call(
        functools.partial(update_kernel, count, source.shape[0], count - len(c)),
        out_shape=jax.ShapeDtypeStruct((rows, cols), F32),
        grid_spec=pltpu.PrefetchScalarGridSpec(
            num_scalar_prefetch=1,
            grid=(rows // step,),
            in_specs=[pl.BlockSpec((step, depth), along)] * count
            + [pl.BlockSpec((cols, depth), fixed)] * len(c)
            + [pl.BlockSpec(x.shape, fixed) for x in pieces]
            + [
                pl.BlockSpec((step, cols), along),
                pl.BlockSpec((step, 1), along),
                pl.BlockSpec((1, cols), fixed),
            ],
            out_specs=pl.BlockSpec((step, cols), along),
            scratch_shapes=[pltpu.VMEM((cols, 3 * count * depth), BF16)],
        ),
        compiler_params=pltpu.CompilerParams(vmem_limit_bytes=VMEM),
        cost_estimate=pl.CostEstimate(
            flops=6 * rows * cols * depth * count, bytes_accessed=8 * rows * cols, transcendentals=0
        ),
        name="update" if ring is None else "finish",
    )(source, *m, *c, *pieces, acc, row_gap, col_gap)


def shards(t_amps, cholesky, eps_occ, eps_vir):
    rows, cols = t_amps.shape
    nrow, ncol = lax.axis_size("row"), lax.axis_size("col")
    blk, chol = cholesky.shape
    width = chol // CHUNKS
    r, z = lax.axis_index("row"), lax.axis_index("col")
    tie = lax.optimization_barrier

    pair = jnp.arange(rows)[:, None] - z * blk
    t_one = t_amps + ((pair == jnp.arange(cols)[None, :] - r * blk) & (pair >= 0) & (pair < blk)).astype(F32)
    gaps = (eps_vir[None, :] - eps_occ[:, None]).reshape(nrow * rows)
    row_gap = lax.dynamic_slice_in_dim(gaps, r * rows, rows, 0).reshape(rows, 1)
    col_gap = lax.dynamic_slice_in_dim(gaps.reshape(nrow, ncol, blk), z, 1, 1).reshape(1, cols)

    mine, other, source, (t_one, cholesky) = ring_gather(cholesky[:, :width], nrow, (t_one, cholesky))
    pieces = jnp.concatenate([mine, other], axis=0)
    l = jnp.concatenate(
        [lax.dynamic_slice_in_dim(pieces, source[i] * blk, blk, 0) for i in range(nrow)], axis=0
    )
    factor, start = {0: (l, 0)}, 1
    for count in GROUPS:
        l = row_gather(cholesky[:, start * width : (start + count) * width])
        factor.update({start + k: (l, k * width) for k in range(count)})
        start += count

    def multiply(c, t):
        l, offset = factor[c]
        return mul(t, l[:, offset : offset + width], ((1,), (0,)))

    part_of = {0: tie(multiply(0, t_one))}
    steps = CHUNKS + ncol - 2

    def at(k):
        return part_of[min(max(k, 0), max(part_of))]

    def going_up(s):
        term = pick(z, [at(s - i) for i in range(ncol)])
        return term + up[-1] if up else term

    def going_down(s):
        term = pick(z, [at(s - (ncol - 1 - i)) for i in range(ncol)])
        return term + down[-1] if down else term

    up, down, partial, m_rows, m_cols, due = [], [], {}, {}, {}, {}

    def arrive(c, term, s, above, below):
        if 0 <= s - c <= ncol - 2:
            term = term + jnp.where(z == s - c + 1, above, 0.0) + jnp.where(z == c + ncol - 2 - s, below, 0.0)
        return term

    def own_rows(x):
        return lax.dynamic_slice_in_dim(x, z * blk, blk, 0)

    def taken(chunks):
        return [m_rows[c] for c in chunks], [m_cols[c] for c in chunks]

    out, used = None, 0
    above = going_up(0)
    for s in range(steps):
        below = going_down(s)
        c = s - (ncol - 1)
        came = (up[-1], down[-1]) if up else None
        if s < CHUNKS:
            partial[s] = part_of[s]
        span = range(0)
        if used == 0 and len(m_cols) >= FIRST:
            span = range(FIRST)
        elif used and len(m_cols) > used:
            span = range(used, len(m_cols))
        kept = [m_rows[k] for k in span]
        above, below, t, came, kept = tie((above, below, t_one, came, kept))
        live = [i for i in range(ncol - 1) if 0 <= s - i < CHUNKS]
        up.append(lax.ppermute(above, "col", [(i, i + 1) for i in live]))
        down.append(lax.ppermute(below, "col", [(ncol - 1 - i, ncol - 2 - i) for i in live]))
        work = {}
        if s + 1 < CHUNKS:
            work["part"] = multiply(s + 1, t)
        if came is not None:
            work["partial"] = {k: arrive(k, x, s - 1, *came) for k, x in partial.items() if k < s}
        if s == 1:
            work["gaps"] = (row_gap, col_gap)
        if s in due:
            work["cols"] = due[s][1]
        if span:
            used = span[-1] + 1
            cols_of = [m_cols[k] for k in span]
            if out is None:
                a, b = jnp.concatenate(kept, axis=1), jnp.concatenate(cols_of, axis=1)
                out = mul(a, b, ((1,), (1,)))
            else:
                out = update(out, kept, cols_of)
            work["out"] = out
        up[-1], work = tie((up[-1], work))
        partial.update(work.get("partial", {}))
        row_gap, col_gap = work.get("gaps", (row_gap, col_gap))
        if "part" in work:
            part_of[s + 1] = work["part"]
        above = going_up(s + 1) if s + 1 < steps else None
        own = own_rows(partial[c]) if 0 <= c and s < steps - 1 else None
        down[-1], above, own = tie((down[-1], above, own))
        if c >= 0:
            m_rows[c] = partial.pop(c)
        if own is not None:
            due[s + LAG] = (c, row_gather(own))
        if "cols" in work:
            m_cols[due.pop(s)[0]] = work["cols"]
        out = work.get("out", out)
    end = CHUNKS - 1
    given = (partial[end], up[-1], down[-1])
    own = arrive(end, own_rows(given[0]), steps - 1, own_rows(up[-1]), own_rows(down[-1]))
    own, given = tie((jnp.concatenate([own_rows(m_rows[end - 1]), own], axis=1), given))
    for c, l in due.values():
        m_cols[c] = l
    *ring, out = ring_gather(own, nrow, update(out, *taken(range(used, end - 2))))
    m_rows[end] = arrive(end, given[0], steps - 1, *given[1:])
    return update(out, [m_rows[c] for c in range(end - 2, end + 1)], [m_cols[end - 2]], ring, row_gap, col_gap)


def solution(mesh):
    in_specs = (P("row", "col"), P(("row", "col"), None), P(), P())
    out_specs = P("row", "col")
    return jax.shard_map(shards, mesh=mesh, in_specs=in_specs, out_specs=out_specs, check_vma=False)
```
